32 devices in a mesh: cent: 4 (over y, x), rows: 8 (over z, core).
Axes of the slice: x: 2, y: 2, z: 4, core: 2. Of those that a mesh axis runs over, the one named last changes fastest.
Arguments:
- embeddings: bfloat16 [8192, 2048], P(('cent', 'rows')), may hold values from -6 to 6
- centroids: bfloat16 [4096, 2048], P(('cent', 'rows')), may hold values from -0.125 to 0.125
- cluster: int32 [8192, 1], P(('cent', 'rows')), may hold values from 0 to 31; in each aligned block of 256 rows (0 to 255, 256 to 511, ...) at most 16 rows name the same one
- noise_salt: int32 [1], replicated, may hold values from 0 to 1048575
Outputs:
- perturbed_max: float32 [8192], P(('cent', 'rows'))
- dedup_score: float32 [8192], P(('cent', 'rows'))
- new_centroids: float32 [32, 2048], P(('cent', 'rows'))
The draws below stay inside these ranges and needn't reach their ends.
Inputs may be any that keep to these rules, and one draw needn't show every extreme that they name: In every aligned block of 256 rows (the rows of one device) no cluster is named by more than 16 rows, and in some block some cluster by exactly 16; every cluster is named by some row.
All inputs are finite; a program needn't handle non-finite values.
Results may differ from the reference program's by a relative error of at most 0.0003.
Values may be sent and summed in bfloat16 or wider, within the bound.
No kernel may reach another device: no remote copies, remote signals or barrier semaphores. Data moves between devices by JAX's collectives and lax.ppermute only.
A program may use at most 128 MiB of HBM per device.

```python
import math
import jax
import jax.numpy as jnp
import numpy as np
from jax import lax

D = 2048
ROWS_DEV = 256
R = 8192
K = 4096
CLUSTERS = 32
MOST = 16
DEVICES = 32


def level_of(stream_key, dims, cuts, least, largest):
    level, own = 1.0, jax.random.fold_in(stream_key, 6)
    for position, blocks in cuts:
        heights = jnp.exp(jax.random.uniform(jax.random.fold_in(own, position), (blocks,), jnp.float32, least / len(cuts), largest / len(cuts)))
        level = level * jnp.repeat(heights, dims[position] // blocks).reshape([-1 if axis == position else 1 for axis in range(len(dims))])
    return level


def shared_out(rng, own, number, rows, count, top, most, lean):
    sequence = jax.random.permutation(rng, count)
    crowded, common = portions_of(count, rows * top, most, lean, True), portions_of(count, rows * top, most, lean, False)
    places = jnp.arange(count)

    def named(tallies, offset_by):
        used = int((tallies > 0).sum())
        fixed = max(1, used // 4)
        passed = fixed + (places - fixed + offset_by * (used - fixed)) % max(1, count - fixed)
        return jnp.zeros((count,), jnp.int32).at[sequence[jnp.where(places < fixed, places, passed)]].set(jnp.asarray(tallies, jnp.int32))

    tallies = jnp.where(number % 4 == 0, named(crowded, number // 4), named(common, number - number // 4 - 1))
    mixed = jax.random.permutation(jax.random.fold_in(own, 3), count)
    giver, sink = mixed[0:count // 2 * 2:2], mixed[1:count // 2 * 2:2]
    room = jnp.minimum(tallies[giver] - 1, most - tallies[sink]) // 2
    room = jnp.where((giver == sequence[0]) | (sink == sequence[0]) | (tallies[sink] == 0), 0, jnp.maximum(room, 0))
    passed = jax.random.randint(jax.random.fold_in(own, 4), (count // 2,), 0, 1 << 20) % (room + 1)
    tallies = tallies.at[giver].add(-passed).at[sink].add(passed)
    items = jnp.searchsorted(jnp.cumsum(tallies), jnp.arange(rows * top), side="right").astype(jnp.int32)
    table = items.reshape(top, rows).T
    table = table[jax.random.permutation(jax.random.fold_in(own, 1), rows)]
    offset_by = jax.random.randint(jax.random.fold_in(own, 2), (rows, 1), 0, top)
    return jnp.take_along_axis(table, (jnp.arange(top)[None, :] + offset_by) % top, axis=1)


def portions_of(count, total, most, skew, full):
    weights = [(1 << 20) // math.isqrt(standing ** skew) + 1 for standing in range(1, count + 1)]
    largest = most if full else min(most, max(-(-total // count), total * weights[0] // sum(weights)))
    least = 1 if total - largest >= count - 1 else 0
    counts, surplus = [largest] + [least] * (count - 1), total - largest - least * (count - 1)
    while surplus > 0:
        movable = [i for i in range(1, count) if counts[i] < largest] or [i for i in range(1, count) if counts[i] < most]
        whole, budget = sum([weights[i] for i in movable]), surplus
        for i in movable:
            more = min(most - counts[i], max(1, budget * weights[i] // whole), surplus)
            counts[i] = counts[i] + more
            surplus = surplus - more
    return np.array(counts)


def centred(key, extent, scale, limit, shards=(), held_as=jnp.bfloat16):
    values = scale * jax.random.normal(key, extent, jnp.float32)
    if shards:
        values = values * level_of(key, extent, shards, -0.22, 0.18)
    return jnp.clip(values, -limit, limit).astype(held_as)


def setup_inputs(seed: int = 0) -> dict:
    splits = jax.random.split(jax.random.key(seed), 5)
    embeddings = centred(splits[0], (R, D), 1.0, 6.0, ((0, 32),))
    centroids = centred(splits[1], (K, D), D ** -0.5, 0.125, ((0, 32),))
    cluster_keys = jax.random.split(jax.random.fold_in(splits[2], 1), R // ROWS_DEV)
    cluster_turns = jax.random.permutation(jax.random.fold_in(splits[2], 3), R // ROWS_DEV)
    cluster = jax.vmap(lambda own, number: shared_out(jax.random.fold_in(splits[2], 2), own, number, ROWS_DEV, CLUSTERS, 1, MOST, 2))(cluster_keys, cluster_turns).reshape((R, 1))
    noise_salt = jax.random.randint(splits[3], (1,), 0, 1048576).astype(jnp.int32)
    return {"embeddings": embeddings, "centroids": centroids, "cluster": cluster, "noise_salt": noise_salt}


inverse_temp = 3.0
epsilon = 1e-06

def logical_shift(word, amount):
    return lax.shift_right_logical(word, jnp.full(word.shape, amount, jnp.int32))

def gumbel_noise(row_ids, cent_ids, salt_word):
    mixed = (row_ids * 1103515245 + cent_ids * 739982445 + salt_word).astype(jnp.int32)
    mixed = mixed ^ logical_shift(mixed, 16)
    mixed = (mixed * 2146121005).astype(jnp.int32)
    mixed = mixed ^ logical_shift(mixed, 15)
    mixed = (mixed * 1759714725).astype(jnp.int32)
    mixed = mixed ^ logical_shift(mixed, 16)
    low_bits = mixed & 8388607
    uniform = (low_bits.astype(jnp.float32) + 0.5) * (1.0 / 8388608.0)
    return -jnp.log(-jnp.log(uniform))

def cluster_stats(members, valid):
    feature_dim = members.shape[1]
    widened = members.astype(jnp.float32)
    scale = lax.rsqrt(lax.optimization_barrier(jnp.mean(widened * widened, axis=1)) + epsilon)
    gram = lax.dot_general(members, members, (((1,), (1,)), ((), ())), preferred_element_type=jnp.float32)
    similar = gram * scale[:, None] * scale[None, :] * (1.0 / math.sqrt(feature_dim))
    order = jnp.arange(members.shape[0], dtype=jnp.int32)
    usable = valid[None, :] & (order[:, None] != order[None, :])
    highest = lax.optimization_barrier(jnp.max(jnp.where(usable, similar, -1e+30), axis=1))
    scores = jnp.where(jnp.any(usable, axis=1), highest, 0.0)
    total = lax.optimization_barrier(jnp.sum(jnp.where(valid[:, None], widened, 0.0), axis=0))
    center = total * lax.rsqrt(jnp.mean(total * total) + epsilon)
    return (scores, center)

def reference(embeddings, centroids, cluster, noise_salt):
    total_rows = embeddings.shape[0]
    cent_ids = jnp.arange(centroids.shape[0], dtype=jnp.int32)
    block = math.gcd(total_rows, 1024)

    def score_rows(start):
        rows_block = lax.dynamic_slice_in_dim(embeddings, start, block, 0)
        scores = lax.dot_general(rows_block, centroids, (((1,), (1,)), ((), ())), preferred_element_type=jnp.float32)
        row_ids = start + jnp.arange(block, dtype=jnp.int32)
        perturbed = inverse_temp * scores + gumbel_noise(row_ids[:, None], cent_ids[None, :], noise_salt[0])
        return lax.optimization_barrier(jnp.max(perturbed, axis=1))
    starts = jnp.arange(total_rows // block, dtype=jnp.int32) * block
    perturbed_max = lax.map(score_rows, starts).reshape(total_rows)
    assigned = cluster[:, 0].reshape(DEVICES, ROWS_DEV)
    order = jnp.arange(ROWS_DEV, dtype=jnp.int32)
    same = (assigned[:, :, None] == assigned[:, None, :]) & (order[None, None, :] < order[None, :, None])
    rank = lax.optimization_barrier(jnp.sum(same.astype(jnp.int32), axis=2))
    sources = jnp.broadcast_to(jnp.arange(DEVICES, dtype=jnp.int32)[:, None], (DEVICES, ROWS_DEV))
    row_index = jnp.arange(total_rows, dtype=jnp.int32).reshape(DEVICES, ROWS_DEV)
    table = jnp.full((CLUSTERS, DEVICES, MOST), total_rows, jnp.int32).at[assigned, sources, rank].set(row_index)

    def one_cluster(entries):
        valid = entries < total_rows
        members = embeddings[jnp.minimum(entries, total_rows - 1)]
        members = jnp.where(valid[:, None], members, jnp.zeros((), embeddings.dtype))
        return cluster_stats(members, valid)
    scores, centers = lax.map(one_cluster, table.reshape(CLUSTERS, DEVICES * MOST))
    dedup_score = jnp.zeros((total_rows,), jnp.float32).at[table.reshape(-1)].set(scores.reshape(-1), mode='drop')
    return (perturbed_max, dedup_score, centers)
```

```python
import math

import jax
import jax.numpy as jnp
from jax import lax
from jax.experimental import pallas as pl
from jax.experimental.pallas import tpu as pltpu
from jax.sharding import PartitionSpec as P

inverse_temp = 3.0
epsilon = 1e-06


def logical_shift(word, amount):
    return lax.shift_right_logical(word, jnp.full(word.shape, amount, jnp.int32))


def gumbel_noise(row_ids, cent_ids, salt_word):
    mixed = row_ids * 1103515245 + cent_ids * 739982445 + salt_word
    mixed = mixed ^ logical_shift(mixed, 16)
    mixed = mixed * 2146121005
    mixed = mixed ^ logical_shift(mixed, 15)
    mixed = mixed * 1759714725
    mixed = mixed ^ logical_shift(mixed, 16)
    low_bits = mixed & 8388607
    uniform = (low_bits.astype(jnp.float32) + 0.5) * (1.0 / 8388608.0)
    return -jnp.log(-jnp.log(uniform))


def cluster_stats(members, valid):
    feature_dim = members.shape[1]
    widened = members.astype(jnp.float32)
    scale = lax.rsqrt(jnp.mean(widened * widened, axis=1) + epsilon)
    gram = lax.dot_general(
        members, members, (((1,), (1,)), ((), ())), preferred_element_type=jnp.float32
    )
    similar = gram * scale[:, None] * scale[None, :] * (1.0 / math.sqrt(feature_dim))
    order = jnp.arange(members.shape[0], dtype=jnp.int32)
    usable = valid[None, :] & (order[:, None] != order[None, :])
    highest = jnp.max(jnp.where(usable, similar, -1e30), axis=1)
    scores = jnp.where(jnp.any(usable, axis=1), highest, 0.0)
    total = jnp.sum(jnp.where(valid[:, None], widened, 0.0), axis=0)
    center = total * lax.rsqrt(jnp.mean(total * total) + epsilon)
    return (scores, center)


def shards(embeddings, centroids, cluster, noise_salt):
    rows_dev, feature_dim = embeddings.shape
    cent_dev = centroids.shape[0]
    cent_count = lax.axis_size("cent")
    rows_count = lax.axis_size("rows")
    devices = cent_count * rows_count
    capacity = max(2, 2 * rows_dev // devices)
    cent_index = lax.axis_index("cent")
    rows_index = lax.axis_index("rows")
    salt_word = noise_salt[0]
    group = lax.all_gather(embeddings, "cent", axis=0, tiled=True)
    position = jnp.arange(cent_count * rows_dev, dtype=jnp.int32)
    group_ids = (position // rows_dev * rows_count + rows_index) * rows_dev + position % rows_dev
    panel_base = cent_index * (rows_count * cent_dev)
    initial = jnp.full((cent_count * rows_dev,), -1e30, jnp.float32)
    piece = lax.all_gather(centroids, "rows", axis=0, tiled=True)
    piece_rows = piece.shape[0]
    block = math.gcd(piece_rows, 512)
    tiles = piece.reshape(piece_rows // block, block, feature_dim)
    offsets = jnp.arange(piece_rows // block, dtype=jnp.int32) * block

    def step(carry, item):
        tile, offset = item
        scores = lax.dot_general(
            group, tile, (((1,), (1,)), ((), ())), preferred_element_type=jnp.float32
        )
        cent_ids = panel_base + offset + jnp.arange(block, dtype=jnp.int32)
        perturbed = inverse_temp * scores + gumbel_noise(
            group_ids[:, None], cent_ids[None, :], salt_word
        )
        return (jnp.maximum(carry, jnp.max(perturbed, axis=1)), None)

    result, unused = lax.scan(step, initial, (tiles, offsets))
    merged = lax.pmax(result, "cent")
    perturbed_max = lax.dynamic_slice_in_dim(merged, cent_index * rows_dev, rows_dev)
    assigned = cluster[:, 0]
    order = jnp.arange(rows_dev, dtype=jnp.int32)
    same = (assigned[:, None] == assigned[None, :]) & (order[None, :] < order[:, None])
    rank = jnp.sum(same.astype(jnp.int32), axis=1)
    slot = assigned * capacity + rank
    outgoing = jnp.zeros((devices * capacity, feature_dim), jnp.bfloat16).at[slot].set(embeddings)
    present = (
        jnp.zeros((devices * capacity,), jnp.bfloat16)
        .at[slot]
        .set(jnp.ones((rows_dev,), jnp.bfloat16))
    )
    received, arrived = (
        lax.all_to_all(
            outgoing.reshape(devices, capacity, feature_dim),
            ("cent", "rows"),
            split_axis=0,
            concat_axis=0,
            tiled=True,
        ),
        lax.all_to_all(
            present.reshape(devices, capacity),
            ("cent", "rows"),
            split_axis=0,
            concat_axis=0,
            tiled=True,
        ),
    )
    members = received.reshape(devices * capacity, feature_dim)
    valid = arrived.reshape(devices * capacity) > 0.5
    scores, center = cluster_stats(members, valid)
    returned = lax.all_to_all(
        scores.reshape(devices, capacity), ("cent", "rows"), split_axis=0, concat_axis=0, tiled=True
    )
    dedup_score = returned.reshape(devices * capacity)[slot]
    return (perturbed_max, dedup_score, center[None, :])


lowest = -1e30
VMEM = pl.BlockSpec(memory_space=pltpu.VMEM)
SMEM = pl.BlockSpec(memory_space=pltpu.SMEM)


def product(left, right):
    return lax.dot_general(left, right, (((1,), (1,)), ((), ())), preferred_element_type=jnp.float32)


def top(values):
    return jnp.max(values, axis=0, keepdims=True)


def read_note(note):
    words = note[:, 0:1024].astype(jnp.float32)
    scale = words[:, 256:512] + words[:, 512:768] + words[:, 768:1024]
    return words[:, 0:256], scale


def as_columns(note):
    cluster, scale = read_note(note)
    return cluster.T[:, 0:1], scale.T[:, 0:1]


def note_kernel(emb, cluster, own_out, scale_out):
    rows = emb.shape[0]
    total = jnp.zeros((rows, 128), jnp.float32)
    for at in range(0, emb.shape[1], 128):
        piece = emb[:, at : at + 128]
        own_out[pl.ds(0, rows), at : at + 128] = piece
        piece = piece.astype(jnp.float32)
        total = total + piece * piece
    mean = jnp.sum(total.T, axis=0, keepdims=True) * (1.0 / emb.shape[1])
    scale = lax.rsqrt(mean + epsilon)
    scale_out[...] = scale
    high = scale.astype(jnp.bfloat16)
    rest = scale - high.astype(jnp.float32)
    middle = rest.astype(jnp.bfloat16)
    low = (rest - middle.astype(jnp.float32)).astype(jnp.bfloat16)
    named = cluster[...].astype(jnp.float32).astype(jnp.bfloat16)
    zeros = jnp.zeros((8, 1024), jnp.bfloat16)
    line = jnp.concatenate([named, high, middle, low], axis=1)
    own_out[pl.ds(rows, 8), :] = jnp.concatenate([jnp.broadcast_to(line, (8, 1024)), zeros], axis=1)


def blocks_of(whole, split):
    pieces = [(ref, 0, 256) for ref in whole]
    notes = [ref[pl.ds(256, 8), :] for ref in whole]
    for first, second in split:
        pieces += [(first, 128, 128), (second, 128, 128)]
        notes.append(second[pl.ds(256, 8), :])
    return pieces, notes


def stack(pieces):
    return jnp.concatenate([ref[pl.ds(lo, rows), :] for ref, lo, rows in pieces], axis=0)


def write_columns(columns, notes):
    for index, note in enumerate(notes):
        rows = pl.ds(256 * index, 256)
        for lo, value in zip((0, 128), as_columns(note)):
            columns[rows, lo : lo + 128] = jnp.broadcast_to(value, (256, 128))


def read_columns(columns):
    return tuple(jnp.concatenate([columns[:, lo : lo + 128]] * 2, axis=1) for lo in (0, 128))


def similarity(pieces, columns, rows, cluster, same=False):
    grams = product(stack(pieces), rows)
    of_cluster, scale = read_columns(columns)
    usable = of_cluster == cluster
    if same:
        shape = grams.shape
        usable = usable & (lax.broadcasted_iota(jnp.int32, shape, 0) != lax.broadcasted_iota(jnp.int32, shape, 1))
    return top(jnp.where(usable, grams * scale, lowest))


def sums_of(pos, pieces, notes):
    named = jnp.concatenate([read_note(note)[0][0:1] for note in notes], axis=1)
    owned = pos[0] * 8 + 2 * lax.broadcasted_iota(jnp.int32, (8, named.shape[1]), 0) + pos[1] % 2
    chosen = (owned.astype(jnp.float32) == named).astype(jnp.bfloat16)
    return jnp.dot(chosen, stack(pieces), preferred_element_type=jnp.float32)


def named_rows(ref):
    return ref[pl.ds(0, 256), :], read_note(ref[pl.ds(256, 8), :])[0][0:1]


def choose(target, first, second, pos):
    layer = pos[1] // 2
    mid = (layer == 1) | (layer == 2)

    @pl.when(mid)
    def _():
        target[...] = first[...]

    @pl.when(jnp.logical_not(mid))
    def _():
        target[...] = second[...]

    return mid


def in_the_middle(pos):
    layer = pos[1] // 2
    return (layer == 1) | (layer == 2)


def early_kernel(pos, own, own_s, gx, gx_s, x0, m1, sims, sums, columns):
    pieces, notes = blocks_of((own, own_s, gx, gx_s), ())
    write_columns(columns, notes)
    for number, ref in enumerate((own, x0)):
        sims[number] = similarity(pieces, columns, *named_rows(ref), same=number == 0)
    sims[2] = jnp.full((1, 256), lowest, jnp.float32)

    @pl.when(in_the_middle(pos))
    def _():
        sims[2] = similarity(pieces, columns, *named_rows(m1))

    sums[...] = sums_of(pos, pieces, notes)


def first_kernel(
    pos, own, own_s, gx, gx_s, gy, gy_s, hx, hx_s, hy, hy_s, cents, cents_s, x0, m1, x1, m3, noise, noise_far, early,
    early_sums, early_columns, result, sums, columns, near,
):
    mid = choose(near, m1, x1, pos)
    pieces, notes = blocks_of((gy, gy_s), ((hy, hx), (hy_s, hx_s)))
    write_columns(columns, notes)
    before = blocks_of((own, own_s, gx, gx_s), ())[0]
    cent_pieces = [(ref, 0, 128) for ref in (cents, cents_s, hx, hx_s, hy, hy_s)]
    for number, ref in enumerate((own, x0, near)):
        rows, cluster = named_rows(ref)
        sim = similarity(pieces, columns, rows, cluster)
        lanes = slice(256 * number, 256 * number + 256)
        score = top(inverse_temp * product(stack(cent_pieces), rows) + noise[:, lanes])
        result[number] = jnp.concatenate([score, jnp.maximum(sim, early[number])], axis=0)
    sums[...] = early_sums[...] + sums_of(pos, pieces, notes)

    @pl.when(mid)
    def _():
        rows, cluster = named_rows(m3)
        sim = jnp.maximum(similarity(before, early_columns, rows, cluster), similarity(pieces, columns, rows, cluster))
        score = top(inverse_temp * product(stack(cent_pieces), rows) + noise_far[0:768, :])
        result[3] = jnp.concatenate([score, sim], axis=0)

    @pl.when(jnp.logical_not(mid))
    def _():
        sim = similarity(before, early_columns, *named_rows(near))
        result[2] = jnp.concatenate([result[2][0:1], jnp.maximum(result[2][1:2], sim)], axis=0)


def whole_visit(rows, cluster, layer_refs, columns, noise):
    own, own_s, gx, gx_s, gy, gy_s, hx, hx_s, hy, hy_s, cents, cents_s, d, d_s = layer_refs
    first = blocks_of((own, own_s, gx, gx_s), ())[0]
    second = blocks_of((gy, gy_s), ((hy, hx), (hy_s, hx_s)))[0]
    sim = similarity(first, columns[0], rows, cluster)
    sim = jnp.maximum(sim, similarity(second, columns[1], rows, cluster))
    pieces = [(ref, 0, 128) for ref in (cents, cents_s, hx, hx_s, hy, hy_s, d, d_s)]
    return top(inverse_temp * product(stack(pieces), rows) + noise[...]), sim


def second_kernel(
    pos, own, x0, m1, x1, m3, d, d_s, noise, noise_far, before, sums, mine, by_one, by_two, by_three, near,
):
    mid = choose(near, m1, x1, pos)
    layer = pos[1] // 2
    cents = stack([(d, 0, 128), (d_s, 0, 128)])

    def visit(number, ref, values):
        score = top(inverse_temp * product(cents, ref[pl.ds(0, 256), :]) + values)
        return jnp.maximum(score, before[number][0:1]), before[number][1:2]

    results = [visit(i, ref, noise[:, 256 * i : 256 * i + 256]) for i, ref in enumerate((own, x0, near))]
    mine[:, 0:256], mine[:, 256:512] = results[0]
    by_one[:, 0:256], by_one[:, 256:512] = results[1]
    for bits, out in ((0, mine), (1, by_one), (2, by_two), (3, by_three)):
        out[:, 512:] = sums[pl.ds(layer ^ bits, 1), :]

    @pl.when(mid)
    def _():
        by_three[:, 0:256], by_three[:, 256:512] = results[2]
        by_two[:, 0:256], by_two[:, 256:512] = visit(3, m3, noise_far[768:1024, :])

    @pl.when(jnp.logical_not(mid))
    def _():
        by_two[:, 0:256], by_two[:, 256:512] = results[2]
        by_three[:, 0:512] = jnp.full((1, 512), lowest, jnp.float32)


def last_kernel(*refs):
    pos, layer_refs, (x2, noise_far), columns, (before, out) = refs[0], refs[1:15], refs[15:17], refs[17:19], refs[19:]
    layer = pos[1] // 2
    out[...] = before[...]

    @pl.when((layer == 0) | (layer == 3))
    def _():
        rows, cluster = named_rows(x2)
        out[:, 0:256], out[:, 256:512] = whole_visit(rows, cluster, layer_refs, columns, noise_far)


def final_kernel(scale, *refs):
    parts, (score_out, sim_out, center_out) = refs[:4], refs[4:]
    score, sim, total = parts[0][:, 0:256], parts[0][:, 256:512], parts[0][:, 512:]
    for part in parts[1:]:
        score = jnp.maximum(score, part[:, 0:256])
        sim = jnp.maximum(sim, part[:, 256:512])
        total = total + part[:, 512:]
    score_out[...] = score
    sim_out[...] = jnp.where(sim > 0.5 * lowest, sim * scale[...] * (1.0 / math.sqrt(total.shape[1])), 0.0)
    center_out[...] = total * lax.rsqrt(jnp.mean(total * total) + epsilon)


def call(kernel, inputs, out_shapes, scratch, flops, mib, scalars=1):
    return pl.pallas_call(
        kernel,
        out_shape=[jax.ShapeDtypeStruct(shape, dtype) for shape, dtype in out_shapes],
        in_specs=[SMEM] * scalars + [VMEM] * (len(inputs) - scalars),
        out_specs=[VMEM] * len(out_shapes),
        scratch_shapes=scratch,
        compiler_params=pltpu.CompilerParams(vmem_limit_bytes=mib * 1024 * 1024),
        cost_estimate=pl.CostEstimate(flops=flops, bytes_accessed=8 * 1024 * 1024, transcendentals=0),
    )(*inputs)


def box_shards(embeddings, centroids, cluster, noise_salt):
    rows_dev, feature_dim = embeddings.shape
    cent_dev = centroids.shape[0]
    cent, row = lax.axis_index("cent"), lax.axis_index("rows")
    layer, core = row // 2, row % 2
    f32, bf16 = jnp.float32, jnp.bfloat16
    pos = jnp.stack([cent, row]).astype(jnp.int32)
    noted = rows_dev + 8

    def along(pairs):
        return [(2 * a + k, 2 * b + k) for a, b in pairs for k in (0, 1)]

    sibling = [(i, i ^ 1) for i in range(8)]
    across = along([(1, 2), (2, 1)]) + sibling[0:2] + sibling[6:8]
    flip = lambda bits: along([(z, z ^ bits) for z in range(4)])
    by_x, by_y = [(i, i ^ 1) for i in range(4)], [(i, i ^ 2) for i in range(4)]
    rows = lambda value, pairs: lax.ppermute(value, "rows", pairs)
    by = lambda value, pairs: lax.ppermute(value, "cent", pairs)
    together = lax.optimization_barrier

    own, scale = call(
        note_kernel,
        [embeddings, cluster.reshape(1, rows_dev)],
        [((noted, feature_dim), bf16), ((1, rows_dev), f32)],
        [],
        rows_dev * feature_dim,
        16,
        0,
    )

    m1, x0, gx, gy = rows(own, across), rows(own, flip(1)), by(own, by_x), by(own, by_y)
    own_s = rows(own, sibling)

    near_row = jnp.where(layer < 2, 4, 2) + core
    far_row = jnp.where(layer < 2, 6, 0) + core
    base = cent * 8

    def ids(devices, count):
        return jnp.concatenate([device * count + jnp.arange(count, dtype=jnp.int32) for device in devices])

    layer_cents = ids([(cent ^ block) * 8 + (row ^ side) for block in range(4) for side in (0, 1)], cent_dev)
    visitors = ids([base + row, base + (row ^ 2), base + near_row, base + far_row], rows_dev)
    noise = lambda row_ids, cent_ids: gumbel_noise(row_ids[None, :], cent_ids[:, None], noise_salt[0])
    noises = [
        noise(visitors[:768], layer_cents[:768]),
        noise(visitors[:768], layer_cents[768:]),
        noise(visitors[768:], layer_cents),
    ]
    m1, x0 = together((m1, x0))
    m3, x1 = rows(x0, across), rows(m1, flip(1))
    gx, gy, own_s, m1, x0, *noises = together((gx, gy, own_s, m1, x0, *noises))

    hx = by(jnp.concatenate([centroids, gy[128:]], axis=0), by_x)
    hy = by(jnp.concatenate([centroids, gx[:128]], axis=0), by_y)
    gx_s = rows(gx, sibling)
    half = 4 * rows_dev
    early = call(
        early_kernel,
        [pos, own, own_s, gx, gx_s, x0, m1],
        [((3, 1, rows_dev), f32), ((8, feature_dim), f32), ((half, 256), f32)],
        [],
        2 * 512 * 1024 * feature_dim,
        16,
    )
    m3, x1, hx, hy, gx_s, gy, cents, *early = together((m3, x1, hx, hy, gx_s, gy, centroids, *early))

    x2, d = rows(m3, flip(1)), by(hx[:128], by_y)
    gy_s, hx_s, hy_s, cents_s = rows(gy, sibling), rows(hx, sibling), rows(hy, sibling), rows(cents, sibling)
    d_s = by(hy_s[:128], by_x)

    layer_pieces = [own, own_s, gx, gx_s, gy, gy_s, hx, hx_s, hy, hy_s, centroids, cents_s]
    one_block = [pltpu.VMEM((noted, feature_dim), bf16)]
    message = ((1, 2 * rows_dev + feature_dim), f32)
    result, sums, columns = call(
        first_kernel,
        [pos] + layer_pieces + [x0, m1, x1, m3, noises[0], noises[2]] + early,
        [((4, 2, rows_dev), f32), ((8, feature_dim), f32), ((half, 256), f32)],
        one_block,
        2 * 256 * 6400 * feature_dim,
        20,
    )
    d, d_s, result = together((d, d_s, result))
    columns = [early[2], columns]
    mine, by_one, by_two, by_three = call(
        second_kernel,
        [pos, own, x0, m1, x1, m3, d, d_s, noises[1], noises[2], result, sums],
        [message] * 4,
        one_block,
        1,
        20,
    )
    one, two = rows(by_one, flip(1)), rows(by_two, flip(2))
    x2, by_three = together((x2, by_three))
    (by_three,) = call(
        last_kernel,
        [pos] + layer_pieces + [d, d_s, x2, noises[2]] + columns + [by_three],
        [message],
        [],
        2 * 256 * 3072 * feature_dim,
        20,
    )
    by_three, one, two = together((by_three, one, two))
    three = rows(by_three, flip(3))
    score, similar, center = call(
        final_kernel,
        [scale, mine, one, two, three],
        [((1, rows_dev), f32), ((1, rows_dev), f32), ((1, feature_dim), f32)],
        [],
        1,
        4,
        0,
    )
    return (score[0], similar[0], center)


def solution(mesh):
    spec = P(("cent", "rows"), None)
    in_specs = (spec, spec, spec, P())
    out_specs = (P(("cent", "rows")), P(("cent", "rows")), spec)
    body = box_shards if dict(mesh.shape) == {"cent": 4, "rows": 8} else shards
    return jax.shard_map(body, mesh=mesh, in_specs=in_specs, out_specs=out_specs, check_vma=False)
```

```python
import math

import jax
import jax.numpy as jnp
from jax import lax
from jax.experimental import pallas as pl
from jax.experimental.pallas import tpu as pltpu
from jax.sharding import PartitionSpec as P

inverse_temp = 3.0
epsilon = 1e-06


def logical_shift(word, amount):
    return lax.shift_right_logical(word, jnp.full(word.shape, amount, jnp.int32))


def gumbel_noise(row_ids, cent_ids, salt_word):
    mixed = row_ids * 1103515245 + cent_ids * 739982445 + salt_word
    mixed = mixed ^ logical_shift(mixed, 16)
    mixed = mixed * 2146121005
    mixed = mixed ^ logical_shift(mixed, 15)
    mixed = mixed * 1759714725
    mixed = mixed ^ logical_shift(mixed, 16)
    low_bits = mixed & 8388607
    uniform = (low_bits.astype(jnp.float32) + 0.5) * (1.0 / 8388608.0)
    return -jnp.log(-jnp.log(uniform))


def cluster_stats(members, valid):
    feature_dim = members.shape[1]
    widened = members.astype(jnp.float32)
    scale = lax.rsqrt(jnp.mean(widened * widened, axis=1) + epsilon)
    gram = lax.dot_general(
        members, members, (((1,), (1,)), ((), ())), preferred_element_type=jnp.float32
    )
    similar = gram * scale[:, None] * scale[None, :] * (1.0 / math.sqrt(feature_dim))
    order = jnp.arange(members.shape[0], dtype=jnp.int32)
    usable = valid[None, :] & (order[:, None] != order[None, :])
    highest = jnp.max(jnp.where(usable, similar, -1e30), axis=1)
    scores = jnp.where(jnp.any(usable, axis=1), highest, 0.0)
    total = jnp.sum(jnp.where(valid[:, None], widened, 0.0), axis=0)
    center = total * lax.rsqrt(jnp.mean(total * total) + epsilon)
    return (scores, center)


def shards(embeddings, centroids, cluster, noise_salt):
    rows_dev, feature_dim = embeddings.shape
    cent_dev = centroids.shape[0]
    cent_count = lax.axis_size("cent")
    rows_count = lax.axis_size("rows")
    devices = cent_count * rows_count
    capacity = max(2, 2 * rows_dev // devices)
    cent_index = lax.axis_index("cent")
    rows_index = lax.axis_index("rows")
    salt_word = noise_salt[0]
    group = lax.all_gather(embeddings, "cent", axis=0, tiled=True)
    position = jnp.arange(cent_count * rows_dev, dtype=jnp.int32)
    group_ids = (position // rows_dev * rows_count + rows_index) * rows_dev + position % rows_dev
    panel_base = cent_index * (rows_count * cent_dev)
    initial = jnp.full((cent_count * rows_dev,), -1e30, jnp.float32)
    piece = lax.all_gather(centroids, "rows", axis=0, tiled=True)
    piece_rows = piece.shape[0]
    block = math.gcd(piece_rows, 512)
    tiles = piece.reshape(piece_rows // block, block, feature_dim)
    offsets = jnp.arange(piece_rows // block, dtype=jnp.int32) * block

    def step(carry, item):
        tile, offset = item
        scores = lax.dot_general(
            group, tile, (((1,), (1,)), ((), ())), preferred_element_type=jnp.float32
        )
        cent_ids = panel_base + offset + jnp.arange(block, dtype=jnp.int32)
        perturbed = inverse_temp * scores + gumbel_noise(
            group_ids[:, None], cent_ids[None, :], salt_word
        )
        return (jnp.maximum(carry, jnp.max(perturbed, axis=1)), None)

    result, unused = lax.scan(step, initial, (tiles, offsets))
    merged = lax.pmax(result, "cent")
    perturbed_max = lax.dynamic_slice_in_dim(merged, cent_index * rows_dev, rows_dev)
    assigned = cluster[:, 0]
    order = jnp.arange(rows_dev, dtype=jnp.int32)
    same = (assigned[:, None] == assigned[None, :]) & (order[None, :] < order[:, None])
    rank = jnp.sum(same.astype(jnp.int32), axis=1)
    slot = assigned * capacity + rank
    outgoing = jnp.zeros((devices * capacity, feature_dim), jnp.bfloat16).at[slot].set(embeddings)
    present = (
        jnp.zeros((devices * capacity,), jnp.bfloat16)
        .at[slot]
        .set(jnp.ones((rows_dev,), jnp.bfloat16))
    )
    received, arrived = (
        lax.all_to_all(
            outgoing.reshape(devices, capacity, feature_dim),
            ("cent", "rows"),
            split_axis=0,
            concat_axis=0,
            tiled=True,
        ),
        lax.all_to_all(
            present.reshape(devices, capacity),
            ("cent", "rows"),
            split_axis=0,
            concat_axis=0,
            tiled=True,
        ),
    )
    members = received.reshape(devices * capacity, feature_dim)
    valid = arrived.reshape(devices * capacity) > 0.5
    scores, center = cluster_stats(members, valid)
    returned = lax.all_to_all(
        scores.reshape(devices, capacity), ("cent", "rows"), split_axis=0, concat_axis=0, tiled=True
    )
    dedup_score = returned.reshape(devices * capacity)[slot]
    return (perturbed_max, dedup_score, center[None, :])


lowest = -1e30
VMEM = pl.BlockSpec(memory_space=pltpu.VMEM)
SMEM = pl.BlockSpec(memory_space=pltpu.SMEM)


def product(left, right):
    return lax.dot_general(left, right, (((1,), (1,)), ((), ())), preferred_element_type=jnp.float32)


def top(values):
    return jnp.max(values, axis=0, keepdims=True)


def read_note(note):
    words = note[:, 0:1024].astype(jnp.float32)
    scale = words[:, 256:512] + words[:, 512:768] + words[:, 768:1024]
    return words[:, 0:256], scale


def as_columns(note):
    cluster, scale = read_note(note)
    return cluster.T[:, 0:1], scale.T[:, 0:1]


def note_kernel(emb, cluster, own_out, scale_out):
    rows = emb.shape[0]
    total = jnp.zeros((rows, 128), jnp.float32)
    for at in range(0, emb.shape[1], 128):
        piece = emb[:, at : at + 128]
        own_out[pl.ds(0, rows), at : at + 128] = piece
        piece = piece.astype(jnp.float32)
        total = total + piece * piece
    mean = jnp.sum(total.T, axis=0, keepdims=True) * (1.0 / emb.shape[1])
    scale = lax.rsqrt(mean + epsilon)
    scale_out[...] = scale
    high = scale.astype(jnp.bfloat16)
    rest = scale - high.astype(jnp.float32)
    middle = rest.astype(jnp.bfloat16)
    low = (rest - middle.astype(jnp.float32)).astype(jnp.bfloat16)
    named = cluster[...].astype(jnp.float32).astype(jnp.bfloat16)
    zeros = jnp.zeros((8, 1024), jnp.bfloat16)
    line = jnp.concatenate([named, high, middle, low], axis=1)
    own_out[pl.ds(rows, 8), :] = jnp.concatenate([jnp.broadcast_to(line, (8, 1024)), zeros], axis=1)


def blocks_of(whole, split):
    pieces = [(ref, 0, 256) for ref in whole]
    notes = [ref[pl.ds(256, 8), :] for ref in whole]
    for first, second in split:
        pieces += [(first, 128, 128), (second, 128, 128)]
        notes.append(second[pl.ds(256, 8), :])
    return pieces, notes


def stack(pieces):
    return jnp.concatenate([ref[pl.ds(lo, rows), :] for ref, lo, rows in pieces], axis=0)


def write_columns(columns, notes):
    for index, note in enumerate(notes):
        rows = pl.ds(256 * index, 256)
        for lo, value in zip((0, 128), as_columns(note)):
            columns[rows, lo : lo + 128] = jnp.broadcast_to(value, (256, 128))


def read_columns(columns):
    return tuple(jnp.concatenate([columns[:, lo : lo + 128]] * 2, axis=1) for lo in (0, 128))


def similarity(pieces, columns, rows, cluster, same=False):
    grams = product(stack(pieces), rows)
    of_cluster, scale = read_columns(columns)
    usable = of_cluster == cluster
    if same:
        shape = grams.shape
        usable = usable & (lax.broadcasted_iota(jnp.int32, shape, 0) != lax.broadcasted_iota(jnp.int32, shape, 1))
    return top(jnp.where(usable, grams * scale, lowest))


def sums_of(pos, pieces, notes):
    named = jnp.concatenate([read_note(note)[0][0:1] for note in notes], axis=1)
    owned = pos[0] * 8 + 2 * lax.broadcasted_iota(jnp.int32, (8, named.shape[1]), 0) + pos[1] % 2
    chosen = (owned.astype(jnp.float32) == named).astype(jnp.bfloat16)
    return jnp.dot(chosen, stack(pieces), preferred_element_type=jnp.float32)


def named_rows(ref):
    return ref[pl.ds(0, 256), :], read_note(ref[pl.ds(256, 8), :])[0][0:1]


def choose(target, first, second, pos):
    layer = pos[1] // 2
    mid = (layer == 1) | (layer == 2)

    @pl.when(mid)
    def _():
        target[...] = first[...]

    @pl.when(jnp.logical_not(mid))
    def _():
        target[...] = second[...]

    return mid


def in_the_middle(pos):
    layer = pos[1] // 2
    return (layer == 1) | (layer == 2)


def early_kernel(pos, own, own_s, gx, gx_s, x0, m1, sims, sums, columns):
    pieces, notes = blocks_of((own, own_s, gx, gx_s), ())
    write_columns(columns, notes)
    for number, ref in enumerate((own, x0)):
        sims[number] = similarity(pieces, columns, *named_rows(ref), same=number == 0)
    sims[2] = jnp.full((1, 256), lowest, jnp.float32)

    @pl.when(in_the_middle(pos))
    def _():
        sims[2] = similarity(pieces, columns, *named_rows(m1))

    sums[...] = sums_of(pos, pieces, notes)


def first_kernel(
    pos, own, own_s, gx, gx_s, gy, gy_s, hx, hx_s, hy, hy_s, cents, cents_s, x0, m1, x1, m3, noise, noise_far, early,
    early_sums, early_columns, result, sums, columns, near,
):
    mid = choose(near, m1, x1, pos)
    pieces, notes = blocks_of((gy, gy_s), ((hy, hx), (hy_s, hx_s)))
    write_columns(columns, notes)
    before = blocks_of((own, own_s, gx, gx_s), ())[0]
    cent_pieces = [(ref, 0, 128) for ref in (cents, cents_s, hx, hx_s, hy, hy_s)]
    for number, ref in enumerate((own, x0, near)):
        rows, cluster = named_rows(ref)
        sim = similarity(pieces, columns, rows, cluster)
        lanes = slice(256 * number, 256 * number + 256)
        score = top(inverse_temp * product(stack(cent_pieces), rows) + noise[:, lanes])
        result[number] = jnp.concatenate([score, jnp.maximum(sim, early[number])], axis=0)
    sums[...] = early_sums[...] + sums_of(pos, pieces, notes)

    @pl.when(mid)
    def _():
        rows, cluster = named_rows(m3)
        sim = jnp.maximum(similarity(before, early_columns, rows, cluster), similarity(pieces, columns, rows, cluster))
        score = top(inverse_temp * product(stack(cent_pieces), rows) + noise_far[0:768, :])
        result[3] = jnp.concatenate([score, sim], axis=0)

    @pl.when(jnp.logical_not(mid))
    def _():
        sim = similarity(before, early_columns, *named_rows(near))
        result[2] = jnp.concatenate([result[2][0:1], jnp.maximum(result[2][1:2], sim)], axis=0)


def whole_visit(rows, cluster, layer_refs, columns, noise):
    own, own_s, gx, gx_s, gy, gy_s, hx, hx_s, hy, hy_s, cents, cents_s, d, d_s = layer_refs
    first = blocks_of((own, own_s, gx, gx_s), ())[0]
    second = blocks_of((gy, gy_s), ((hy, hx), (hy_s, hx_s)))[0]
    sim = similarity(first, columns[0], rows, cluster)
    sim = jnp.maximum(sim, similarity(second, columns[1], rows, cluster))
    pieces = [(ref, 0, 128) for ref in (cents, cents_s, hx, hx_s, hy, hy_s, d, d_s)]
    return top(inverse_temp * product(stack(pieces), rows) + noise[...]), sim


def second_kernel(
    pos, own, x0, m1, x1, m3, d, d_s, noise, noise_far, before, sums, mine, by_one, by_two, by_three, near,
):
    mid = choose(near, m1, x1, pos)
    layer = pos[1] // 2
    cents = stack([(d, 0, 128), (d_s, 0, 128)])

    def visit(number, ref, values):
        score = top(inverse_temp * product(cents, ref[pl.ds(0, 256), :]) + values)
        return jnp.maximum(score, before[number][0:1]), before[number][1:2]

    results = [visit(i, ref, noise[:, 256 * i : 256 * i + 256]) for i, ref in enumerate((own, x0, near))]
    mine[:, 0:256], mine[:, 256:512] = results[0]
    by_one[:, 0:256], by_one[:, 256:512] = results[1]
    for bits, out in ((0, mine), (1, by_one), (2, by_two), (3, by_three)):
        out[:, 512:] = sums[pl.ds(layer ^ bits, 1), :]

    @pl.when(mid)
    def _():
        by_three[:, 0:256], by_three[:, 256:512] = results[2]
        by_two[:, 0:256], by_two[:, 256:512] = visit(3, m3, noise_far[768:1024, :])

    @pl.when(jnp.logical_not(mid))
    def _():
        by_two[:, 0:256], by_two[:, 256:512] = results[2]
        by_three[:, 0:512] = jnp.full((1, 512), lowest, jnp.float32)


def last_kernel(*refs):
    pos, layer_refs, (x2, noise_far), columns, (before, out) = refs[0], refs[1:15], refs[15:17], refs[17:19], refs[19:]
    layer = pos[1] // 2
    out[...] = before[...]

    @pl.when((layer == 0) | (layer == 3))
    def _():
        rows, cluster = named_rows(x2)
        out[:, 0:256], out[:, 256:512] = whole_visit(rows, cluster, layer_refs, columns, noise_far)


def final_kernel(scale, *refs):
    parts, (score_out, sim_out, center_out) = refs[:4], refs[4:]
    score, sim, total = parts[0][:, 0:256], parts[0][:, 256:512], parts[0][:, 512:]
    for part in parts[1:]:
        score = jnp.maximum(score, part[:, 0:256])
        sim = jnp.maximum(sim, part[:, 256:512])
        total = total + part[:, 512:]
    score_out[...] = score
    sim_out[...] = jnp.where(sim > 0.5 * lowest, sim * scale[...] * (1.0 / math.sqrt(total.shape[1])), 0.0)
    center_out[...] = total * lax.rsqrt(jnp.mean(total * total) + epsilon)


def call(kernel, inputs, out_shapes, scratch, flops, mib, scalars=1):
    return pl.pallas_call(
        kernel,
        out_shape=[jax.ShapeDtypeStruct(shape, dtype) for shape, dtype in out_shapes],
        in_specs=[SMEM] * scalars + [VMEM] * (len(inputs) - scalars),
        out_specs=[VMEM] * len(out_shapes),
        scratch_shapes=scratch,
        compiler_params=pltpu.CompilerParams(vmem_limit_bytes=mib * 1024 * 1024),
        cost_estimate=pl.CostEstimate(flops=flops, bytes_accessed=8 * 1024 * 1024, transcendentals=0),
    )(*inputs)


def box_shards(embeddings, centroids, cluster, noise_salt):
    rows_dev, feature_dim = embeddings.shape
    cent_dev = centroids.shape[0]
    cent, row = lax.axis_index("cent"), lax.axis_index("rows")
    layer, core = row // 2, row % 2
    f32, bf16 = jnp.float32, jnp.bfloat16
    pos = jnp.stack([cent, row]).astype(jnp.int32)
    noted = rows_dev + 8

    def along(pairs):
        return [(2 * a + k, 2 * b + k) for a, b in pairs for k in (0, 1)]

    sibling = [(i, i ^ 1) for i in range(8)]
    across = along([(1, 2), (2, 1)]) + sibling[0:2] + sibling[6:8]
    flip = lambda bits: along([(z, z ^ bits) for z in range(4)])
    by_x, by_y = [(i, i ^ 1) for i in range(4)], [(i, i ^ 2) for i in range(4)]
    rows = lambda value, pairs: lax.ppermute(value, "rows", pairs)
    by = lambda value, pairs: lax.ppermute(value, "cent", pairs)
    together = lax.optimization_barrier

    own, scale = call(
        note_kernel,
        [embeddings, cluster.reshape(1, rows_dev)],
        [((noted, feature_dim), bf16), ((1, rows_dev), f32)],
        [],
        rows_dev * feature_dim,
        16,
        0,
    )

    m1, x0, gx, gy = rows(own, across), rows(own, flip(1)), by(own, by_x), by(own, by_y)
    own_s = rows(own, sibling)

    near_row = jnp.where(layer < 2, 4, 2) + core
    far_row = jnp.where(layer < 2, 6, 0) + core
    base = cent * 8

    def ids(devices, count):
        return jnp.concatenate([device * count + jnp.arange(count, dtype=jnp.int32) for device in devices])

    layer_cents = ids([(cent ^ block) * 8 + (row ^ side) for block in range(4) for side in (0, 1)], cent_dev)
    visitors = ids([base + row, base + (row ^ 2), base + near_row, base + far_row], rows_dev)
    noise = lambda row_ids, cent_ids: gumbel_noise(row_ids[None, :], cent_ids[:, None], noise_salt[0])
    noises = [
        noise(visitors[:768], layer_cents[:768]),
        noise(visitors[:768], layer_cents[768:]),
        noise(visitors[768:], layer_cents),
    ]
    m1, x0, *noises = together((m1, x0, *noises))
    m3, x1 = rows(x0, across), rows(m1, flip(1))

    hx = by(jnp.concatenate([centroids, gy[128:]], axis=0), by_x)
    hy = by(jnp.concatenate([centroids, gx[:128]], axis=0), by_y)
    gx_s = rows(gx, sibling)
    half = 4 * rows_dev
    early = call(
        early_kernel,
        [pos, own, own_s, gx, gx_s, x0, m1],
        [((3, 1, rows_dev), f32), ((8, feature_dim), f32), ((half, 256), f32)],
        [],
        2 * 512 * 1024 * feature_dim,
        16,
    )
    m3, x1, gx_s, gy, cents, *early = together((m3, x1, gx_s, gy, centroids, *early))

    x2, d = rows(m3, flip(1)), by(hx[:128], by_y)
    gy_s, hx_s, hy_s, cents_s = rows(gy, sibling), rows(hx, sibling), rows(hy, sibling), rows(cents, sibling)
    d_s = by(hy_s[:128], by_x)

    layer_pieces = [own, own_s, gx, gx_s, gy, gy_s, hx, hx_s, hy, hy_s, centroids, cents_s]
    one_block = [pltpu.VMEM((noted, feature_dim), bf16)]
    message = ((1, 2 * rows_dev + feature_dim), f32)
    result, sums, columns = call(
        first_kernel,
        [pos] + layer_pieces + [x0, m1, x1, m3, noises[0], noises[2]] + early,
        [((4, 2, rows_dev), f32), ((8, feature_dim), f32), ((half, 256), f32)],
        one_block,
        2 * 256 * 6400 * feature_dim,
        20,
    )
    d, d_s, result = together((d, d_s, result))
    columns = [early[2], columns]
    mine, by_one, by_two, by_three = call(
        second_kernel,
        [pos, own, x0, m1, x1, m3, d, d_s, noises[1], noises[2], result, sums],
        [message] * 4,
        one_block,
        1,
        20,
    )
    one, two = rows(by_one, flip(1)), rows(by_two, flip(2))
    x2, by_three = together((x2, by_three))
    (by_three,) = call(
        last_kernel,
        [pos] + layer_pieces + [d, d_s, x2, noises[2]] + columns + [by_three],
        [message],
        [],
        1,
        20,
    )
    by_three, one, two = together((by_three, one, two))
    three = rows(by_three, flip(3))
    score, similar, center = call(
        final_kernel,
        [scale, mine, one, two, three],
        [((1, rows_dev), f32), ((1, rows_dev), f32), ((1, feature_dim), f32)],
        [],
        1,
        4,
        0,
    )
    return (score[0], similar[0], center)


def solution(mesh):
    spec = P(("cent", "rows"), None)
    in_specs = (spec, spec, spec, P())
    out_specs = (P(("cent", "rows")), P(("cent", "rows")), spec)
    body = box_shards if dict(mesh.shape) == {"cent": 4, "rows": 8} else shards
    return jax.shard_map(body, mesh=mesh, in_specs=in_specs, out_specs=out_specs, check_vma=False)
```

```python
import math

import jax
import jax.numpy as jnp
from jax import lax
from jax.experimental import pallas as pl
from jax.experimental.pallas import tpu as pltpu
from jax.sharding import PartitionSpec as P

inverse_temp = 3.0
epsilon = 1e-06


def logical_shift(word, amount):
    return lax.shift_right_logical(word, jnp.full(word.shape, amount, jnp.int32))


def gumbel_noise(row_ids, cent_ids, salt_word):
    mixed = row_ids * 1103515245 + cent_ids * 739982445 + salt_word
    mixed = mixed ^ logical_shift(mixed, 16)
    mixed = mixed * 2146121005
    mixed = mixed ^ logical_shift(mixed, 15)
    mixed = mixed * 1759714725
    mixed = mixed ^ logical_shift(mixed, 16)
    low_bits = mixed & 8388607
    uniform = (low_bits.astype(jnp.float32) + 0.5) * (1.0 / 8388608.0)
    return -jnp.log(-jnp.log(uniform))


def cluster_stats(members, valid):
    feature_dim = members.shape[1]
    widened = members.astype(jnp.float32)
    scale = lax.rsqrt(jnp.mean(widened * widened, axis=1) + epsilon)
    gram = lax.dot_general(
        members, members, (((1,), (1,)), ((), ())), preferred_element_type=jnp.float32
    )
    similar = gram * scale[:, None] * scale[None, :] * (1.0 / math.sqrt(feature_dim))
    order = jnp.arange(members.shape[0], dtype=jnp.int32)
    usable = valid[None, :] & (order[:, None] != order[None, :])
    highest = jnp.max(jnp.where(usable, similar, -1e30), axis=1)
    scores = jnp.where(jnp.any(usable, axis=1), highest, 0.0)
    total = jnp.sum(jnp.where(valid[:, None], widened, 0.0), axis=0)
    center = total * lax.rsqrt(jnp.mean(total * total) + epsilon)
    return (scores, center)


def shards(embeddings, centroids, cluster, noise_salt):
    rows_dev, feature_dim = embeddings.shape
    cent_dev = centroids.shape[0]
    cent_count = lax.axis_size("cent")
    rows_count = lax.axis_size("rows")
    devices = cent_count * rows_count
    capacity = max(2, 2 * rows_dev // devices)
    cent_index = lax.axis_index("cent")
    rows_index = lax.axis_index("rows")
    salt_word = noise_salt[0]
    group = lax.all_gather(embeddings, "cent", axis=0, tiled=True)
    position = jnp.arange(cent_count * rows_dev, dtype=jnp.int32)
    group_ids = (position // rows_dev * rows_count + rows_index) * rows_dev + position % rows_dev
    panel_base = cent_index * (rows_count * cent_dev)
    initial = jnp.full((cent_count * rows_dev,), -1e30, jnp.float32)
    piece = lax.all_gather(centroids, "rows", axis=0, tiled=True)
    piece_rows = piece.shape[0]
    block = math.gcd(piece_rows, 512)
    tiles = piece.reshape(piece_rows // block, block, feature_dim)
    offsets = jnp.arange(piece_rows // block, dtype=jnp.int32) * block

    def step(carry, item):
        tile, offset = item
        scores = lax.dot_general(
            group, tile, (((1,), (1,)), ((), ())), preferred_element_type=jnp.float32
        )
        cent_ids = panel_base + offset + jnp.arange(block, dtype=jnp.int32)
        perturbed = inverse_temp * scores + gumbel_noise(
            group_ids[:, None], cent_ids[None, :], salt_word
        )
        return (jnp.maximum(carry, jnp.max(perturbed, axis=1)), None)

    result, unused = lax.scan(step, initial, (tiles, offsets))
    merged = lax.pmax(result, "cent")
    perturbed_max = lax.dynamic_slice_in_dim(merged, cent_index * rows_dev, rows_dev)
    assigned = cluster[:, 0]
    order = jnp.arange(rows_dev, dtype=jnp.int32)
    same = (assigned[:, None] == assigned[None, :]) & (order[None, :] < order[:, None])
    rank = jnp.sum(same.astype(jnp.int32), axis=1)
    slot = assigned * capacity + rank
    outgoing = jnp.zeros((devices * capacity, feature_dim), jnp.bfloat16).at[slot].set(embeddings)
    present = (
        jnp.zeros((devices * capacity,), jnp.bfloat16)
        .at[slot]
        .set(jnp.ones((rows_dev,), jnp.bfloat16))
    )
    received, arrived = (
        lax.all_to_all(
            outgoing.reshape(devices, capacity, feature_dim),
            ("cent", "rows"),
            split_axis=0,
            concat_axis=0,
            tiled=True,
        ),
        lax.all_to_all(
            present.reshape(devices, capacity),
            ("cent", "rows"),
            split_axis=0,
            concat_axis=0,
            tiled=True,
        ),
    )
    members = received.reshape(devices * capacity, feature_dim)
    valid = arrived.reshape(devices * capacity) > 0.5
    scores, center = cluster_stats(members, valid)
    returned = lax.all_to_all(
        scores.reshape(devices, capacity), ("cent", "rows"), split_axis=0, concat_axis=0, tiled=True
    )
    dedup_score = returned.reshape(devices * capacity)[slot]
    return (perturbed_max, dedup_score, center[None, :])


lowest = -1e30
ANY = pl.BlockSpec(memory_space=pl.ANY)
VMEM = pl.BlockSpec(memory_space=pltpu.VMEM)
SMEM = pl.BlockSpec(memory_space=pltpu.SMEM)


def product(left, right):
    return lax.dot_general(left, right, (((1,), (1,)), ((), ())), preferred_element_type=jnp.float32)


def top(values):
    return jnp.max(values, axis=0, keepdims=True)


def read_note(note):
    words = note[:, 0:1024].astype(jnp.float32)
    scale = words[:, 256:512] + words[:, 512:768] + words[:, 768:1024]
    return words[:, 0:256], scale


def as_columns(note):
    cluster, scale = read_note(note)
    return cluster.T[:, 0:1], scale.T[:, 0:1]


def note_kernel(emb, cluster, own_out, scale_out):
    rows = emb.shape[0]
    total = jnp.zeros((rows, 128), jnp.float32)
    for at in range(0, emb.shape[1], 128):
        piece = emb[:, at : at + 128]
        own_out[pl.ds(0, rows), at : at + 128] = piece
        piece = piece.astype(jnp.float32)
        total = total + piece * piece
    mean = jnp.sum(total.T, axis=0, keepdims=True) * (1.0 / emb.shape[1])
    scale = lax.rsqrt(mean + epsilon)
    scale_out[...] = scale
    high = scale.astype(jnp.bfloat16)
    rest = scale - high.astype(jnp.float32)
    middle = rest.astype(jnp.bfloat16)
    low = (rest - middle.astype(jnp.float32)).astype(jnp.bfloat16)
    named = cluster[...].astype(jnp.float32).astype(jnp.bfloat16)
    zeros = jnp.zeros((8, 1024), jnp.bfloat16)
    line = jnp.concatenate([named, high, middle, low], axis=1)
    own_out[pl.ds(rows, 8), :] = jnp.concatenate([jnp.broadcast_to(line, (8, 1024)), zeros], axis=1)


def blocks_of(whole, split):
    pieces = [(ref, 0, 256) for ref in whole]
    notes = [ref[pl.ds(256, 8), :] for ref in whole]
    for first, second in split:
        pieces += [(first, 128, 128), (second, 128, 128)]
        notes.append(second[pl.ds(256, 8), :])
    return pieces, notes


def stack(pieces):
    return jnp.concatenate([ref[pl.ds(lo, rows), :] for ref, lo, rows in pieces], axis=0)


def write_columns(columns, notes):
    for index, note in enumerate(notes):
        rows = pl.ds(256 * index, 256)
        for lo, value in zip((0, 128), as_columns(note)):
            columns[rows, lo : lo + 128] = jnp.broadcast_to(value, (256, 128))


def read_columns(columns):
    return tuple(jnp.concatenate([columns[:, lo : lo + 128]] * 2, axis=1) for lo in (0, 128))


def similarity(pieces, columns, rows, cluster, same=False):
    grams = product(stack(pieces), rows)
    of_cluster, scale = read_columns(columns)
    usable = of_cluster == cluster
    if same:
        shape = grams.shape
        usable = usable & (lax.broadcasted_iota(jnp.int32, shape, 0) != lax.broadcasted_iota(jnp.int32, shape, 1))
    return top(jnp.where(usable, grams * scale, lowest))


def sums_of(pos, pieces, notes):
    named = jnp.concatenate([read_note(note)[0][0:1] for note in notes], axis=1)
    owned = pos[0] * 8 + 2 * lax.broadcasted_iota(jnp.int32, (8, named.shape[1]), 0) + pos[1] % 2
    chosen = (owned.astype(jnp.float32) == named).astype(jnp.bfloat16)
    return jnp.dot(chosen, stack(pieces), preferred_element_type=jnp.float32)


def named_rows(ref):
    return ref[pl.ds(0, 256), :], read_note(ref[pl.ds(256, 8), :])[0][0:1]


def fetch(source, target, sem):
    copy = pltpu.make_async_copy(source, target, sem)
    copy.start()
    return copy


def fetch_choice(first, second, target, sem, mid):
    @pl.when(mid)
    def _():
        fetch(first, target, sem)

    @pl.when(jnp.logical_not(mid))
    def _():
        fetch(second, target, sem)

    return pltpu.make_async_copy(first, target, sem)


def in_the_middle(pos):
    layer = pos[1] // 2
    return (layer == 1) | (layer == 2)


def early_kernel(pos, own, own_s, gx, gx_s, x0, m1, sims, sums, columns):
    pieces, notes = blocks_of((own, own_s, gx, gx_s), ())
    write_columns(columns, notes)
    for number, ref in enumerate((own, x0)):
        sims[number] = similarity(pieces, columns, *named_rows(ref), same=number == 0)
    sims[2] = jnp.full((1, 256), lowest, jnp.float32)

    @pl.when(in_the_middle(pos))
    def _():
        sims[2] = similarity(pieces, columns, *named_rows(m1))

    sums[...] = sums_of(pos, pieces, notes)


def first_kernel(
    pos, own, own_s, gx, gx_s, gy, gy_s, hx, hx_s, hy, hy_s, cents, cents_s, x0, m1, x1, m3, noise, noise_far, early,
    early_sums, early_columns, result, sums, columns, inner, near, sib, across, sems,
):
    mid = in_the_middle(pos)
    inner_copy = fetch(x0, inner, sems.at[0])
    near_copy = fetch_choice(m1, x1, near, sems.at[1], mid)
    others = [fetch(own_s, sib, sems.at[2]), fetch(gx, across, sems.at[3])]
    pieces, notes = blocks_of((gy, gy_s), ((hy, hx), (hy_s, hx_s)))
    write_columns(columns, notes)
    before = blocks_of((own, sib, across, gx_s), ())[0]
    cent_pieces = [(ref, 0, 128) for ref in (cents, cents_s, hx, hx_s, hy, hy_s)]
    for number, (ref, copy) in enumerate(((own, None), (inner, inner_copy), (near, near_copy))):
        if copy is not None:
            copy.wait()
        rows, cluster = named_rows(ref)
        sim = similarity(pieces, columns, rows, cluster)
        lanes = slice(256 * number, 256 * number + 256)
        score = top(inverse_temp * product(stack(cent_pieces), rows) + noise[:, lanes])
        result[number] = jnp.concatenate([score, jnp.maximum(sim, early[number])], axis=0)
    for copy in others:
        copy.wait()
    sums[...] = early_sums[...] + sums_of(pos, pieces, notes)

    @pl.when(mid)
    def _():
        rows, cluster = named_rows(m3)
        sim = jnp.maximum(similarity(before, early_columns, rows, cluster), similarity(pieces, columns, rows, cluster))
        score = top(inverse_temp * product(stack(cent_pieces), rows) + noise_far[0:768, :])
        result[3] = jnp.concatenate([score, sim], axis=0)

    @pl.when(jnp.logical_not(mid))
    def _():
        sim = similarity(before, early_columns, *named_rows(near))
        result[2] = jnp.concatenate([result[2][0:1], jnp.maximum(result[2][1:2], sim)], axis=0)


def second_kernel(
    pos, own, x0, m1, x1, m3, d, d_s, noise, noise_far, before, sums, mine, by_one, by_two, by_three, inner, near, sems,
):
    mid = in_the_middle(pos)
    copies = [None, fetch(x0, inner, sems.at[0]), fetch_choice(m1, x1, near, sems.at[1], mid)]
    layer = pos[1] // 2
    cents = stack([(d, 0, 128), (d_s, 0, 128)])

    def visit(number, ref, values):
        if number in (1, 2):
            copies[number].wait()
        score = top(inverse_temp * product(cents, ref[pl.ds(0, 256), :]) + values)
        return jnp.maximum(score, before[number][0:1]), before[number][1:2]

    results = [visit(i, ref, noise[:, 256 * i : 256 * i + 256]) for i, ref in enumerate((own, inner, near))]
    mine[:, 0:256], mine[:, 256:512] = results[0]
    by_one[:, 0:256], by_one[:, 256:512] = results[1]
    for bits, out in ((0, mine), (1, by_one), (2, by_two), (3, by_three)):
        out[:, 512:] = sums[pl.ds(layer ^ bits, 1), :]

    @pl.when(mid)
    def _():
        by_three[:, 0:256], by_three[:, 256:512] = results[2]
        by_two[:, 0:256], by_two[:, 256:512] = visit(3, m3, noise_far[768:1024, :])

    @pl.when(jnp.logical_not(mid))
    def _():
        by_two[:, 0:256], by_two[:, 256:512] = results[2]
        by_three[:, 0:512] = jnp.full((1, 512), lowest, jnp.float32)


def last_kernel(
    pos, own, own_s, gx, gx_s, gy, gy_s, hx, hx_s, hy, hy_s, cents, cents_s, d, d_s, x2, noise, early_columns, columns,
    before, out, sib, across, sems,
):
    out[...] = before[...]

    @pl.when(jnp.logical_not(in_the_middle(pos)))
    def _():
        others = [fetch(own_s, sib, sems.at[0]), fetch(gx, across, sems.at[1])]
        rows, cluster = named_rows(x2)
        pieces = [(ref, 0, 128) for ref in (cents, cents_s, hx, hx_s, hy, hy_s, d, d_s)]
        score = top(inverse_temp * product(stack(pieces), rows) + noise[...])
        pieces = blocks_of((gy, gy_s), ((hy, hx), (hy_s, hx_s)))[0]
        sim = similarity(pieces, columns, rows, cluster)
        for copy in others:
            copy.wait()
        pieces = blocks_of((own, sib, across, gx_s), ())[0]
        sim = jnp.maximum(sim, similarity(pieces, early_columns, rows, cluster))
        out[:, 0:256], out[:, 256:512] = score, sim


def final_kernel(scale, *refs):
    parts, (score_out, sim_out, center_out) = refs[:4], refs[4:]
    score, sim, total = parts[0][:, 0:256], parts[0][:, 256:512], parts[0][:, 512:]
    for part in parts[1:]:
        score = jnp.maximum(score, part[:, 0:256])
        sim = jnp.maximum(sim, part[:, 256:512])
        total = total + part[:, 512:]
    score_out[...] = score
    sim_out[...] = jnp.where(sim > 0.5 * lowest, sim * scale[...] * (1.0 / math.sqrt(total.shape[1])), 0.0)
    center_out[...] = total * lax.rsqrt(jnp.mean(total * total) + epsilon)


def call(kernel, inputs, out_shapes, scratch, flops, mib, scalars=1, fetched=()):
    return pl.pallas_call(
        kernel,
        out_shape=[jax.ShapeDtypeStruct(shape, dtype) for shape, dtype in out_shapes],
        in_specs=[SMEM if i < scalars else ANY if i in fetched else VMEM for i in range(len(inputs))],
        out_specs=[VMEM] * len(out_shapes),
        scratch_shapes=scratch,
        compiler_params=pltpu.CompilerParams(vmem_limit_bytes=mib * 1024 * 1024),
        cost_estimate=pl.CostEstimate(flops=flops, bytes_accessed=8 * 1024 * 1024, transcendentals=0),
    )(*inputs)


def box_shards(embeddings, centroids, cluster, noise_salt):
    rows_dev, feature_dim = embeddings.shape
    cent_dev = centroids.shape[0]
    cent, row = lax.axis_index("cent"), lax.axis_index("rows")
    layer, core = row // 2, row % 2
    f32, bf16 = jnp.float32, jnp.bfloat16
    pos = jnp.stack([cent, row]).astype(jnp.int32)
    noted = rows_dev + 8

    def along(pairs):
        return [(2 * a + k, 2 * b + k) for a, b in pairs for k in (0, 1)]

    sibling = [(i, i ^ 1) for i in range(8)]
    across = along([(1, 2), (2, 1)]) + sibling[0:2] + sibling[6:8]
    flip = lambda bits: along([(z, z ^ bits) for z in range(4)])
    by_x, by_y = [(i, i ^ 1) for i in range(4)], [(i, i ^ 2) for i in range(4)]
    rows = lambda value, pairs: lax.ppermute(value, "rows", pairs)
    by = lambda value, pairs: lax.ppermute(value, "cent", pairs)
    together = lax.optimization_barrier

    own, scale = call(
        note_kernel,
        [embeddings, cluster.reshape(1, rows_dev)],
        [((noted, feature_dim), bf16), ((1, rows_dev), f32)],
        [],
        rows_dev * feature_dim,
        16,
        0,
    )

    m1, x0, gx, gy = rows(own, across), rows(own, flip(1)), by(own, by_x), by(own, by_y)
    own_s = rows(own, sibling)

    near_row = jnp.where(layer < 2, 4, 2) + core
    far_row = jnp.where(layer < 2, 6, 0) + core
    base = cent * 8

    def ids(devices, count):
        return jnp.concatenate([device * count + jnp.arange(count, dtype=jnp.int32) for device in devices])

    layer_cents = ids([(cent ^ block) * 8 + (row ^ side) for block in range(4) for side in (0, 1)], cent_dev)
    visitors = ids([base + row, base + (row ^ 2), base + near_row, base + far_row], rows_dev)
    noise = lambda row_ids, cent_ids: gumbel_noise(row_ids[None, :], cent_ids[:, None], noise_salt[0])
    noises = [
        noise(visitors[:768], layer_cents[:768]),
        noise(visitors[:768], layer_cents[768:]),
        noise(visitors[768:], layer_cents),
    ]
    m1, x0, *noises = together((m1, x0, *noises))
    m3, x1 = rows(x0, across), rows(m1, flip(1))

    hx = by(jnp.concatenate([centroids, gy[128:]], axis=0), by_x)
    hy = by(jnp.concatenate([centroids, gx[:128]], axis=0), by_y)
    gx_s = rows(gx, sibling)
    half = 4 * rows_dev
    early = call(
        early_kernel,
        [pos, own, own_s, gx, gx_s, x0, m1],
        [((3, 1, rows_dev), f32), ((8, feature_dim), f32), ((half, 256), f32)],
        [],
        2 * 512 * 1024 * feature_dim,
        16,
    )
    m3, x1, gx_s, gy, cents, *early = together((m3, x1, gx_s, gy, centroids, *early))

    x2, d = rows(m3, flip(1)), by(hx[:128], by_y)
    gy_s, hx_s, hy_s, cents_s = rows(gy, sibling), rows(hx, sibling), rows(hy, sibling), rows(cents, sibling)
    d_s = by(hy_s[:128], by_x)

    layer_pieces = [own, own_s, gx, gx_s, gy, gy_s, hx, hx_s, hy, hy_s, centroids, cents_s]
    blocks = lambda count: [pltpu.VMEM((noted, feature_dim), bf16)] * count + [pltpu.SemaphoreType.DMA((count,))]
    message = ((1, 2 * rows_dev + feature_dim), f32)
    result, sums, columns = call(
        first_kernel,
        [pos] + layer_pieces + [x0, m1, x1, m3, noises[0], noises[2]] + early,
        [((4, 2, rows_dev), f32), ((8, feature_dim), f32), ((half, 256), f32)],
        blocks(4),
        2 * 256 * 6400 * feature_dim,
        20,
        fetched=(2, 3, 13, 14, 15),
    )
    d, d_s, result = together((d, d_s, result))
    columns = [early[2], columns]
    mine, by_one, by_two, by_three = call(
        second_kernel,
        [pos, own, x0, m1, x1, m3, d, d_s, noises[1], noises[2], result, sums],
        [message] * 4,
        blocks(2),
        1,
        20,
        fetched=(2, 3, 4),
    )
    one, two = rows(by_one, flip(1)), rows(by_two, flip(2))
    x2, by_three = together((x2, by_three))
    (by_three,) = call(
        last_kernel,
        [pos] + layer_pieces + [d, d_s, x2, noises[2]] + columns + [by_three],
        [message],
        blocks(2),
        1,
        20,
        fetched=(2, 3),
    )
    by_three, one, two = together((by_three, one, two))
    three = rows(by_three, flip(3))
    score, similar, center = call(
        final_kernel,
        [scale, mine, one, two, three],
        [((1, rows_dev), f32), ((1, rows_dev), f32), ((1, feature_dim), f32)],
        [],
        1,
        4,
        0,
    )
    return (score[0], similar[0], center)


def solution(mesh):
    spec = P(("cent", "rows"), None)
    in_specs = (spec, spec, spec, P())
    out_specs = (P(("cent", "rows")), P(("cent", "rows")), spec)
    body = box_shards if dict(mesh.shape) == {"cent": 4, "rows": 8} else shards
    return jax.shard_map(body, mesh=mesh, in_specs=in_specs, out_specs=out_specs, check_vma=False)
```

```python
import math

import jax
import jax.numpy as jnp
from jax import lax
from jax.experimental import pallas as pl
from jax.experimental.pallas import tpu as pltpu
from jax.sharding import PartitionSpec as P

inverse_temp = 3.0
epsilon = 1e-06


def logical_shift(word, amount):
    return lax.shift_right_logical(word, jnp.full(word.shape, amount, jnp.int32))


def gumbel_noise(row_ids, cent_ids, salt_word):
    mixed = row_ids * 1103515245 + cent_ids * 739982445 + salt_word
    mixed = mixed ^ logical_shift(mixed, 16)
    mixed = mixed * 2146121005
    mixed = mixed ^ logical_shift(mixed, 15)
    mixed = mixed * 1759714725
    mixed = mixed ^ logical_shift(mixed, 16)
    low_bits = mixed & 8388607
    uniform = (low_bits.astype(jnp.float32) + 0.5) * (1.0 / 8388608.0)
    return -jnp.log(-jnp.log(uniform))


def cluster_stats(members, valid):
    feature_dim = members.shape[1]
    widened = members.astype(jnp.float32)
    scale = lax.rsqrt(jnp.mean(widened * widened, axis=1) + epsilon)
    gram = lax.dot_general(
        members, members, (((1,), (1,)), ((), ())), preferred_element_type=jnp.float32
    )
    similar = gram * scale[:, None] * scale[None, :] * (1.0 / math.sqrt(feature_dim))
    order = jnp.arange(members.shape[0], dtype=jnp.int32)
    usable = valid[None, :] & (order[:, None] != order[None, :])
    highest = jnp.max(jnp.where(usable, similar, -1e30), axis=1)
    scores = jnp.where(jnp.any(usable, axis=1), highest, 0.0)
    total = jnp.sum(jnp.where(valid[:, None], widened, 0.0), axis=0)
    center = total * lax.rsqrt(jnp.mean(total * total) + epsilon)
    return (scores, center)


def shards(embeddings, centroids, cluster, noise_salt):
    rows_dev, feature_dim = embeddings.shape
    cent_dev = centroids.shape[0]
    cent_count = lax.axis_size("cent")
    rows_count = lax.axis_size("rows")
    devices = cent_count * rows_count
    capacity = max(2, 2 * rows_dev // devices)
    cent_index = lax.axis_index("cent")
    rows_index = lax.axis_index("rows")
    salt_word = noise_salt[0]
    group = lax.all_gather(embeddings, "cent", axis=0, tiled=True)
    position = jnp.arange(cent_count * rows_dev, dtype=jnp.int32)
    group_ids = (position // rows_dev * rows_count + rows_index) * rows_dev + position % rows_dev
    panel_base = cent_index * (rows_count * cent_dev)
    initial = jnp.full((cent_count * rows_dev,), -1e30, jnp.float32)
    piece = lax.all_gather(centroids, "rows", axis=0, tiled=True)
    piece_rows = piece.shape[0]
    block = math.gcd(piece_rows, 512)
    tiles = piece.reshape(piece_rows // block, block, feature_dim)
    offsets = jnp.arange(piece_rows // block, dtype=jnp.int32) * block

    def step(carry, item):
        tile, offset = item
        scores = lax.dot_general(
            group, tile, (((1,), (1,)), ((), ())), preferred_element_type=jnp.float32
        )
        cent_ids = panel_base + offset + jnp.arange(block, dtype=jnp.int32)
        perturbed = inverse_temp * scores + gumbel_noise(
            group_ids[:, None], cent_ids[None, :], salt_word
        )
        return (jnp.maximum(carry, jnp.max(perturbed, axis=1)), None)

    result, unused = lax.scan(step, initial, (tiles, offsets))
    merged = lax.pmax(result, "cent")
    perturbed_max = lax.dynamic_slice_in_dim(merged, cent_index * rows_dev, rows_dev)
    assigned = cluster[:, 0]
    order = jnp.arange(rows_dev, dtype=jnp.int32)
    same = (assigned[:, None] == assigned[None, :]) & (order[None, :] < order[:, None])
    rank = jnp.sum(same.astype(jnp.int32), axis=1)
    slot = assigned * capacity + rank
    outgoing = jnp.zeros((devices * capacity, feature_dim), jnp.bfloat16).at[slot].set(embeddings)
    present = (
        jnp.zeros((devices * capacity,), jnp.bfloat16)
        .at[slot]
        .set(jnp.ones((rows_dev,), jnp.bfloat16))
    )
    received, arrived = (
        lax.all_to_all(
            outgoing.reshape(devices, capacity, feature_dim),
            ("cent", "rows"),
            split_axis=0,
            concat_axis=0,
            tiled=True,
        ),
        lax.all_to_all(
            present.reshape(devices, capacity),
            ("cent", "rows"),
            split_axis=0,
            concat_axis=0,
            tiled=True,
        ),
    )
    members = received.reshape(devices * capacity, feature_dim)
    valid = arrived.reshape(devices * capacity) > 0.5
    scores, center = cluster_stats(members, valid)
    returned = lax.all_to_all(
        scores.reshape(devices, capacity), ("cent", "rows"), split_axis=0, concat_axis=0, tiled=True
    )
    dedup_score = returned.reshape(devices * capacity)[slot]
    return (perturbed_max, dedup_score, center[None, :])


lowest = -1e30
HEAD = 32
VMEM = pl.BlockSpec(memory_space=pltpu.VMEM)
SMEM = pl.BlockSpec(memory_space=pltpu.SMEM)


def product(left, right):
    return lax.dot_general(left, right, (((1,), (1,)), ((), ())), preferred_element_type=jnp.float32)


def top(values):
    return jnp.max(values, axis=0, keepdims=True)


def read_note(note):
    words = note[:, 0:1024].astype(jnp.float32)
    scale = words[:, 256:512] + words[:, 512:768] + words[:, 768:1024]
    return words[:, 0:256], scale


def as_columns(note):
    cluster, scale = read_note(note)
    return cluster.T[:, 0:1], scale.T[:, 0:1]


def note_kernel(emb, cluster, own_out, scale_out):
    rows = emb.shape[0]
    total = jnp.zeros((rows, 128), jnp.float32)
    for at in range(0, emb.shape[1], 128):
        piece = emb[:, at : at + 128]
        own_out[pl.ds(0, rows), at : at + 128] = piece
        piece = piece.astype(jnp.float32)
        total = total + piece * piece
    mean = jnp.sum(total.T, axis=0, keepdims=True) * (1.0 / emb.shape[1])
    scale = lax.rsqrt(mean + epsilon)
    scale_out[...] = scale
    high = scale.astype(jnp.bfloat16)
    rest = scale - high.astype(jnp.float32)
    middle = rest.astype(jnp.bfloat16)
    low = (rest - middle.astype(jnp.float32)).astype(jnp.bfloat16)
    named = cluster[...].astype(jnp.float32).astype(jnp.bfloat16)
    zeros = jnp.zeros((8, 1024), jnp.bfloat16)
    line = jnp.concatenate([named, high, middle, low], axis=1)
    own_out[pl.ds(rows, 8), :] = jnp.concatenate([jnp.broadcast_to(line, (8, 1024)), zeros], axis=1)


def blocks_of(whole, split):
    pieces = [(ref, 0, 256) for ref in whole]
    notes = [ref[pl.ds(256, 8), :] for ref in whole]
    for first, second in split:
        pieces += [(first, 128, 128), (second, 128, 128)]
        notes.append(second[pl.ds(256, 8), :])
    return pieces, notes


def stack(pieces):
    return jnp.concatenate([ref[pl.ds(lo, rows), :] for ref, lo, rows in pieces], axis=0)


def write_columns(columns, notes):
    for index, note in enumerate(notes):
        rows = pl.ds(256 * index, 256)
        for lo, value in zip((0, 128), as_columns(note)):
            columns[rows, lo : lo + 128] = jnp.broadcast_to(value, (256, 128))


def read_columns(columns):
    return tuple(jnp.concatenate([columns[:, lo : lo + 128]] * 2, axis=1) for lo in (0, 128))


def similarity(pieces, columns, rows, cluster, same=False):
    grams = product(stack(pieces), rows)
    of_cluster, scale = read_columns(columns)
    usable = of_cluster == cluster
    if same:
        shape = grams.shape
        usable = usable & (lax.broadcasted_iota(jnp.int32, shape, 0) != lax.broadcasted_iota(jnp.int32, shape, 1))
    return top(jnp.where(usable, grams * scale, lowest))


def sums_of(pos, pieces, notes):
    named = jnp.concatenate([read_note(note)[0][0:1] for note in notes], axis=1)
    owned = pos[0] * 8 + 2 * lax.broadcasted_iota(jnp.int32, (8, named.shape[1]), 0) + pos[1] % 2
    chosen = (owned.astype(jnp.float32) == named).astype(jnp.bfloat16)
    return jnp.dot(chosen, stack(pieces), preferred_element_type=jnp.float32)


def named_rows(ref):
    return ref[pl.ds(0, 256), :], read_note(ref[pl.ds(256, 8), :])[0][0:1]


def choose(target, first, second, pos):
    layer = pos[1] // 2
    mid = (layer == 1) | (layer == 2)

    @pl.when(mid)
    def _():
        target[...] = first[...]

    @pl.when(jnp.logical_not(mid))
    def _():
        target[...] = second[...]

    return mid


def in_the_middle(pos):
    layer = pos[1] // 2
    return (layer == 1) | (layer == 2)


def early_kernel(pos, own, own_s, gx, gx_s, x0, m1, sims, sums, columns):
    pieces, notes = blocks_of((own, own_s, gx, gx_s), ())
    write_columns(columns, notes)
    for number, ref in enumerate((own, x0)):
        sims[number] = similarity(pieces, columns, *named_rows(ref), same=number == 0)
    sims[2] = jnp.full((1, 256), lowest, jnp.float32)

    @pl.when(in_the_middle(pos))
    def _():
        sims[2] = similarity(pieces, columns, *named_rows(m1))

    sums[...] = sums_of(pos, pieces, notes)


def first_kernel(
    pos, own, own_s, gx, gx_s, gy, gy_s, hx, hx_s, hy, hy_s, cents, cents_s, x0, m1, x1, m3, noise, noise_far, early,
    early_sums, early_columns, result, sums, columns, near,
):
    mid = choose(near, m1, x1, pos)
    pieces, notes = blocks_of((gy, gy_s), ((hy, hx), (hy_s, hx_s)))
    write_columns(columns, notes)
    before = blocks_of((own, own_s, gx, gx_s), ())[0]
    cent_pieces = [(ref, 0, 128) for ref in (cents, cents_s, hx, hx_s, hy, hy_s)]
    for number, ref in enumerate((own, x0, near)):
        rows, cluster = named_rows(ref)
        sim = similarity(pieces, columns, rows, cluster)
        lanes = slice(256 * number, 256 * number + 256)
        score = top(inverse_temp * product(stack(cent_pieces), rows) + noise[:, lanes])
        result[number] = jnp.concatenate([score, jnp.maximum(sim, early[number])], axis=0)
    sums[...] = early_sums[...] + sums_of(pos, pieces, notes)

    @pl.when(mid)
    def _():
        rows, cluster = named_rows(m3)
        sim = jnp.maximum(similarity(before, early_columns, rows, cluster), similarity(pieces, columns, rows, cluster))
        score = top(inverse_temp * product(stack(cent_pieces), rows) + noise_far[0:768, :])
        result[3] = jnp.concatenate([score, sim], axis=0)

    @pl.when(jnp.logical_not(mid))
    def _():
        sim = similarity(before, early_columns, *named_rows(near))
        result[2] = jnp.concatenate([result[2][0:1], jnp.maximum(result[2][1:2], sim)], axis=0)


def second_kernel(
    pos, own, x0, m1, x1, m3, d, d_s, noise, noise_far, before, sums, mine, by_one, by_two, by_three, near,
):
    mid = choose(near, m1, x1, pos)
    layer = pos[1] // 2
    cents = stack([(d, 0, 128), (d_s, 0, 128)])

    def visit(number, ref, values):
        score = top(inverse_temp * product(cents, ref[pl.ds(0, 256), :]) + values)
        return jnp.maximum(score, before[number][0:1]), before[number][1:2]

    results = [visit(i, ref, noise[:, 256 * i : 256 * i + 256]) for i, ref in enumerate((own, x0, near))]
    mine[:, 0:256], mine[:, 256:512] = results[0]
    by_one[:, 0:256], by_one[:, 256:512] = results[1]
    for bits, out in ((0, mine), (1, by_one), (2, by_two), (3, by_three)):
        out[:, 512:] = sums[pl.ds(layer ^ bits, 1), :]

    @pl.when(mid)
    def _():
        by_three[:, 0:256], by_three[:, 256:512] = results[2]
        by_two[:, 0:256], by_two[:, 256:512] = visit(3, m3, noise_far[768:1024, :])

    @pl.when(jnp.logical_not(mid))
    def _():
        by_two[:, 0:256], by_two[:, 256:512] = results[2]
        by_three[:, 0:512] = jnp.full((1, 512), lowest, jnp.float32)


def last_kernel(
    pos, own, own_s, gx, gx_s, gy, gy_s, hx, hx_s, hy, hy_s, cents, cents_s, d, d_s, head, tail, noise, early_columns,
    columns, before, out,
):
    out[...] = before[...]

    @pl.when(jnp.logical_not(in_the_middle(pos)))
    def _():
        rows = jnp.concatenate([head[...], tail[pl.ds(0, 256 - HEAD), :]], axis=0)
        cluster = read_note(tail[pl.ds(256 - HEAD, 8), :])[0][0:1]
        first = blocks_of((own, own_s, gx, gx_s), ())[0]
        second = blocks_of((gy, gy_s), ((hy, hx), (hy_s, hx_s)))[0]
        sim = similarity(first, early_columns, rows, cluster)
        out[:, 256:512] = jnp.maximum(sim, similarity(second, columns, rows, cluster))
        pieces = [(ref, 0, 128) for ref in (cents, cents_s, hx, hx_s, hy, hy_s, d, d_s)]
        out[:, 0:256] = top(inverse_temp * product(stack(pieces), rows) + noise[...])


def final_kernel(scale, *refs):
    parts, (score_out, sim_out, center_out) = refs[:4], refs[4:]
    score, sim, total = parts[0][:, 0:256], parts[0][:, 256:512], parts[0][:, 512:]
    for part in parts[1:]:
        score = jnp.maximum(score, part[:, 0:256])
        sim = jnp.maximum(sim, part[:, 256:512])
        total = total + part[:, 512:]
    score_out[...] = score
    sim_out[...] = jnp.where(sim > 0.5 * lowest, sim * scale[...] * (1.0 / math.sqrt(total.shape[1])), 0.0)
    center_out[...] = total * lax.rsqrt(jnp.mean(total * total) + epsilon)


def call(kernel, inputs, out_shapes, scratch, flops, mib, scalars=1):
    return pl.pallas_call(
        kernel,
        out_shape=[jax.ShapeDtypeStruct(shape, dtype) for shape, dtype in out_shapes],
        in_specs=[SMEM] * scalars + [VMEM] * (len(inputs) - scalars),
        out_specs=[VMEM] * len(out_shapes),
        scratch_shapes=scratch,
        compiler_params=pltpu.CompilerParams(vmem_limit_bytes=mib * 1024 * 1024),
        cost_estimate=pl.CostEstimate(flops=flops, bytes_accessed=8 * 1024 * 1024, transcendentals=0),
    )(*inputs)


def box_shards(embeddings, centroids, cluster, noise_salt):
    rows_dev, feature_dim = embeddings.shape
    cent_dev = centroids.shape[0]
    cent, row = lax.axis_index("cent"), lax.axis_index("rows")
    layer, core = row // 2, row % 2
    f32, bf16 = jnp.float32, jnp.bfloat16
    pos = jnp.stack([cent, row]).astype(jnp.int32)
    noted = rows_dev + 8

    def along(pairs):
        return [(2 * a + k, 2 * b + k) for a, b in pairs for k in (0, 1)]

    sibling = [(i, i ^ 1) for i in range(8)]
    across = along([(1, 2), (2, 1)]) + sibling[0:2] + sibling[6:8]
    between_ends = along([(0, 3), (3, 0)]) + sibling[2:6]
    flip = lambda bits: along([(z, z ^ bits) for z in range(4)])
    by_x, by_y = [(i, i ^ 1) for i in range(4)], [(i, i ^ 2) for i in range(4)]
    rows = lambda value, pairs: lax.ppermute(value, "rows", pairs)
    by = lambda value, pairs: lax.ppermute(value, "cent", pairs)
    together = lax.optimization_barrier

    own, scale = call(
        note_kernel,
        [embeddings, cluster.reshape(1, rows_dev)],
        [((noted, feature_dim), bf16), ((1, rows_dev), f32)],
        [],
        rows_dev * feature_dim,
        16,
        0,
    )

    m1, x0, gx, gy = rows(own, across), rows(own, flip(1)), by(own, by_x), by(own, by_y)
    own_s = rows(own, sibling)

    near_row = jnp.where(layer < 2, 4, 2) + core
    far_row = jnp.where(layer < 2, 6, 0) + core
    base = cent * 8

    def ids(devices, count):
        return jnp.concatenate([device * count + jnp.arange(count, dtype=jnp.int32) for device in devices])

    layer_cents = ids([(cent ^ block) * 8 + (row ^ side) for block in range(4) for side in (0, 1)], cent_dev)
    visitors = ids([base + row, base + (row ^ 2), base + near_row, base + far_row], rows_dev)
    noise = lambda row_ids, cent_ids: gumbel_noise(row_ids[None, :], cent_ids[:, None], noise_salt[0])
    noises = [
        noise(visitors[:768], layer_cents[:768]),
        noise(visitors[:768], layer_cents[768:]),
        noise(visitors[768:], layer_cents),
    ]
    m1, x0, head, *noises = together((m1, x0, own[:HEAD], *noises))
    m3, x1 = rows(x0, across), rows(m1, flip(1))
    far_head = rows(head, between_ends)

    hx = by(jnp.concatenate([centroids, gy[128:]], axis=0), by_x)
    hy = by(jnp.concatenate([centroids, gx[:128]], axis=0), by_y)
    gx_s = rows(gx, sibling)
    half = 4 * rows_dev
    early = call(
        early_kernel,
        [pos, own, own_s, gx, gx_s, x0, m1],
        [((3, 1, rows_dev), f32), ((8, feature_dim), f32), ((half, 256), f32)],
        [],
        2 * 512 * 1024 * feature_dim,
        16,
    )
    m3, x1, far_head, far_tail, gx_s, gy, cents, *early = together((m3, x1, far_head, own[HEAD:], gx_s, gy, centroids, *early))

    far_tail, d = rows(far_tail, between_ends), by(hx[:128], by_y)
    gy_s, hx_s, hy_s, cents_s = rows(gy, sibling), rows(hx, sibling), rows(hy, sibling), rows(cents, sibling)
    d_s = by(hy_s[:128], by_x)

    layer_pieces = [own, own_s, gx, gx_s, gy, gy_s, hx, hx_s, hy, hy_s, centroids, cents_s]
    one_block = [pltpu.VMEM((noted, feature_dim), bf16)]
    message = ((1, 2 * rows_dev + feature_dim), f32)
    result, sums, columns = call(
        first_kernel,
        [pos] + layer_pieces + [x0, m1, x1, m3, noises[0], noises[2]] + early,
        [((4, 2, rows_dev), f32), ((8, feature_dim), f32), ((half, 256), f32)],
        one_block,
        2 * 256 * 6400 * feature_dim,
        20,
    )
    d, d_s, result = together((d, d_s, result))
    columns = [early[2], columns]
    mine, by_one, by_two, by_three = call(
        second_kernel,
        [pos, own, x0, m1, x1, m3, d, d_s, noises[1], noises[2], result, sums],
        [message] * 4,
        one_block,
        1,
        20,
    )
    one, two = rows(by_one, flip(1)), rows(by_two, flip(2))
    far_tail, by_three = together((far_tail, by_three))
    (by_three,) = call(
        last_kernel,
        [pos] + layer_pieces + [d, d_s, far_head, far_tail, noises[2]] + columns + [by_three],
        [message],
        [],
        1,
        20,
    )
    by_three, one, two = together((by_three, one, two))
    three = rows(by_three, flip(3))
    score, similar, center = call(
        final_kernel,
        [scale, mine, one, two, three],
        [((1, rows_dev), f32), ((1, rows_dev), f32), ((1, feature_dim), f32)],
        [],
        1,
        4,
        0,
    )
    return (score[0], similar[0], center)


def solution(mesh):
    spec = P(("cent", "rows"), None)
    in_specs = (spec, spec, spec, P())
    out_specs = (P(("cent", "rows")), P(("cent", "rows")), spec)
    body = box_shards if dict(mesh.shape) == {"cent": 4, "rows": 8} else shards
    return jax.shard_map(body, mesh=mesh, in_specs=in_specs, out_specs=out_specs, check_vma=False)
```
